256 devices in a mesh: grp: 4 (over z_hi, core), pos: 64 (over z_lo, x, y).
Axes of the slice: x: 4, y: 4, z: 8 (z_hi: 2, z_lo: 4; z = z_hi * 4 + z_lo), core: 2. Of those that a mesh axis runs over, the one named last changes fastest.
Arguments:
- query: float32 [256, 131072], P(None, ('grp', 'pos')), may hold values from -6 to 6
- key_branch: float32 [256, 131072], P(None, ('grp', 'pos')), may hold values from -6 to 6
- value_branch: float32 [256, 131072], P(None, ('grp', 'pos')), may hold values from -6 to 6
- long_filter: float32 [256, 131072], P(None, ('grp', 'pos')), may hold values from -0.015625 to 0.015625
- skip_gain: float32 [256], replicated, may hold values from -4 to 4
Outputs:
- mixed: float32 [256, 131072], P(None, ('grp', 'pos'))
The draws below stay inside these ranges and needn't reach their ends.
All inputs are finite; a program needn't handle non-finite values.
Results may differ from the reference program's by a relative error of at most 0.000062.
Values sent between devices are 32-bit elements; how exact they have to be, the bound alone decides.
No kernel may reach another device: no remote copies, remote signals or barrier semaphores. Data moves between devices by JAX's collectives and lax.ppermute only.
A program may use at most 64 MiB of HBM per device.

```python
import jax
import jax.numpy as jnp

CHANNELS = 256
LEN = 131072


def levels(own_key, extent, shards, low, top_value):
    def one(axis_at, parts):
        draws = jax.random.uniform(jax.random.fold_in(jax.random.fold_in(own_key, 6), axis_at), (parts,), jnp.float32, low / len(shards), top_value / len(shards))
        return jnp.repeat(jnp.exp(draws), extent[axis_at] // parts).reshape((-1,) + (1,) * (len(extent) - axis_at - 1))

    factor_of = one(*shards[0])
    for cut in shards[1:]:
        factor_of = factor_of * one(*cut)
    return factor_of


def bell_draw(rng, extent, deviation, most, pieces=(), dtype=jnp.bfloat16):
    gain = levels(rng, extent, pieces, -0.22, 0.18) if pieces else 1.0
    drawn = jax.random.normal(rng, extent, jnp.float32) * deviation * gain
    return jnp.minimum(jnp.maximum(drawn, -most), most).astype(dtype)


def setup_inputs(seed: int = 0) -> dict:
    streams_of = jax.random.split(jax.random.key(seed), 6)
    query = bell_draw(streams_of[0], (CHANNELS, LEN), 1.0, 6.0, ((1, 256),), jnp.float32)
    key_branch = bell_draw(streams_of[1], (CHANNELS, LEN), 1.0, 6.0, ((1, 256),), jnp.float32)
    value_branch = bell_draw(streams_of[2], (CHANNELS, LEN), 1.0, 6.0, ((1, 256),), jnp.float32)
    long_filter = bell_draw(streams_of[3], (CHANNELS, LEN), LEN ** -0.5, 0.015625, ((1, 256),), jnp.float32)
    skip_gain = bell_draw(streams_of[4], (CHANNELS,), 1.0, 4.0, (), jnp.float32)
    return {"query": query, "key_branch": key_branch, "value_branch": value_branch, "long_filter": long_filter, "skip_gain": skip_gain}


def reference(query, key_branch, value_branch, long_filter, skip_gain):
    gated_input = key_branch * value_branch
    spectrum_in = jnp.fft.rfft(gated_input, n=2 * LEN, axis=1)
    spectrum_filter = jnp.fft.rfft(long_filter, n=2 * LEN, axis=1)
    convolved = jnp.fft.irfft(spectrum_in * spectrum_filter, n=2 * LEN, axis=1)[:, :LEN]
    return query * (convolved + skip_gain[:, None] * gated_input)
```

```python
import numpy as np

import jax
import jax.numpy as jnp
from jax import lax
from jax.sharding import PartitionSpec as P

AXES = ("grp", "pos")


def turns(numerator, denominator):
    angle = 2.0 * np.pi * (numerator % denominator) / denominator
    return np.cos(angle), np.sin(angle)


def tables(lines, width):
    length = lines * width
    line = np.arange(lines)
    offset = np.arange(width)
    c1, s1 = turns(np.outer(4 * line + 1, line), 4 * lines)
    ct, st = turns(np.outer(4 * line + 1, offset), 4 * length)
    c2, s2 = turns(np.outer(offset, offset), width)
    first = np.concatenate([c1, -s1], 0)
    second = np.block([[c2, -s2], [s2, c2]])
    back_second = np.block([[c2, s2], [-s2, c2]]) / length
    back_first = np.concatenate([c1.T, -s1.T], 1)
    return [a.astype(np.float32) for a in (first, ct, st, second, back_second, back_first)]


def dot(a, b):
    return jnp.dot(a, b, precision=lax.Precision.HIGH, preferred_element_type=jnp.float32)


def body(query, key_branch, value_branch, long_filter, skip_gain):
    channels, width = query.shape
    lines = lax.axis_size("grp") * lax.axis_size("pos")
    first, ct, st, second, back_second, back_first = tables(lines, width)
    gated = key_branch * value_branch
    both = jnp.concatenate(
        [gated.reshape(channels, width // 128, 128), long_filter.reshape(channels, width // 128, 128)], 1
    )
    both = lax.all_to_all(both, AXES, split_axis=0, concat_axis=0, tiled=True)
    both = both.reshape(lines, 2 * width)
    spread = dot(first, both)
    real, imag = spread[:lines], spread[lines:]
    cc, ss = jnp.tile(ct, (1, 2)), jnp.tile(st, (1, 2))
    real, imag = real * cc + imag * ss, imag * cc - real * ss
    rows = jnp.concatenate([real, imag], 1)
    rows = rows.reshape(lines, 2, 2, width).transpose(2, 0, 1, 3).reshape(2 * lines, 2 * width)
    spectra = dot(rows, second)
    ar, ai = spectra[:lines, :width], spectra[:lines, width:]
    br, bi = spectra[lines:, :width], spectra[lines:, width:]
    product = jnp.concatenate([ar * br - ai * bi, ar * bi + ai * br], 1)
    back = dot(product, back_second)
    real, imag = back[:, :width], back[:, width:]
    real, imag = real * ct - imag * st, imag * ct + real * st
    convolved = dot(back_first, jnp.concatenate([real, imag], 0))
    convolved = lax.all_to_all(
        convolved.reshape(lines, width // 128, 128), AXES, split_axis=0, concat_axis=0, tiled=True
    ).reshape(channels, width)
    return query * (convolved + skip_gain[:, None] * gated)


def solution(mesh):
    return jax.shard_map(
        body,
        mesh=mesh,
        in_specs=(P(None, AXES), P(None, AXES), P(None, AXES), P(None, AXES), P()),
        out_specs=P(None, AXES),
        check_vma=False,
    )
```

```python
import functools

import ml_dtypes
import numpy as np

import jax
import jax.numpy as jnp
from jax import lax
from jax.experimental import pallas as pl
from jax.experimental.pallas import tpu as pltpu
from jax.sharding import PartitionSpec as P

AXES = ("grp", "pos")
LANES = 128
RADIX = 4
PARAMS = pltpu.CompilerParams(vmem_limit_bytes=40 * 2**20)


def turns(numerator, denominator):
    angle = 2.0 * np.pi * (numerator % denominator) / denominator
    return np.cos(angle), np.sin(angle)


def high_low(table):
    high = table.astype(ml_dtypes.bfloat16)
    low = (table - high.astype(np.float64)).astype(ml_dtypes.bfloat16)
    return high, low


def left_table(table):
    high, low = high_low(table)
    return np.concatenate([high, low, high], -1)


def right_table(table):
    high, low = high_low(table)
    return np.concatenate([high, low, high], -2)


@functools.lru_cache
def tables(lines, width):
    length = lines * width
    line = np.arange(lines)
    offset = np.arange(width)
    c1, s1 = turns(np.outer(4 * line + 1, line), 4 * lines)
    ct, st = turns(np.outer(4 * line + 1, offset), 4 * length)
    small = np.arange(width // RADIX)
    forth, back = [], []
    for r in range(RADIX):
        c2, s2 = turns(np.outer(small, RADIX * small + r), width)
        block = np.block([[c2, -s2], [s2, c2]])
        forth.append(block)
        back.append(block.T / length)
    return (
        left_table(np.concatenate([c1, -s1], 0)),
        np.concatenate([ct, st], 0).astype(np.float32),
        right_table(np.stack(forth)),
        right_table(np.stack(back)),
        left_table(np.concatenate([c1.T, -s1.T], 1)),
    )


def split(x):
    high = x.astype(jnp.bfloat16)
    return high, (x - high.astype(jnp.float32)).astype(jnp.bfloat16)


def dot(a, b):
    return jnp.dot(a, b, preferred_element_type=jnp.float32)


def gate_kernel(key_ref, value_ref, filter_ref, out_ref):
    channels, width = key_ref.shape
    blocks = width // LANES
    for q in range(blocks):
        at = pl.ds(q * LANES, LANES)
        out_ref[pl.ds(q, channels, stride=2 * blocks), :] = key_ref[:, at] * value_ref[:, at]
        out_ref[pl.ds(blocks + q, channels, stride=2 * blocks), :] = filter_ref[:, at]


def convolve_kernel(x_ref, first_ref, twist_ref, forth_ref, back_ref, last_ref, y_ref, xs, a, zh, zl, c, dh, dl):
    lines = y_ref.shape[0] // RADIX
    width = RADIX * LANES
    step = 32
    for j in range(2 * RADIX):
        high, low = split(x_ref[pl.ds(j, lines, stride=2 * RADIX), :])
        at = pl.ds(j * LANES, LANES)
        xs[0:lines, at] = high
        xs[lines : 2 * lines, at] = high
        xs[2 * lines : 3 * lines, at] = low
    for n in range(0, 2 * width, 256):
        a[:, n : n + 256] = dot(first_ref[...], xs[:, n : n + 256])
    for signal in range(2):
        for row in range(0, lines, step):
            re, im = [], []
            for q in range(RADIX):
                at = slice(signal * width + q * LANES, signal * width + (q + 1) * LANES)
                ar, ai = a[row : row + step, at], a[lines + row : lines + row + step, at]
                at = slice(q * LANES, (q + 1) * LANES)
                ct, st = twist_ref[row : row + step, at], twist_ref[lines + row : lines + row + step, at]
                re.append(ar * ct + ai * st)
                im.append(ai * ct - ar * st)
            e0r, e0i, e1r, e1i = re[0] + re[2], im[0] + im[2], re[0] - re[2], im[0] - im[2]
            o0r, o0i, o1r, o1i = re[1] + re[3], im[1] + im[3], re[1] - re[3], im[1] - im[3]
            outs = (
                (e0r + o0r, e0i + o0i),
                (e1r + o1i, e1i - o1r),
                (e0r - o0r, e0i - o0i),
                (e1r - o1i, e1i + o1r),
            )
            rows = slice(signal * lines + row, signal * lines + row + step)
            for r, pair in enumerate(outs):
                for part, value in enumerate(pair):
                    high, low = split(value)
                    at = slice(part * LANES, (part + 1) * LANES)
                    zh[r, rows, at] = high
                    zl[r, rows, at] = low
    for r in range(RADIX):
        high = zh[r]
        spectra = dot(jnp.concatenate([high, high, zl[r]], 1), forth_ref[r])
        gr, gi = spectra[:lines, :LANES], spectra[:lines, LANES:]
        fr, fi = spectra[lines:, :LANES], spectra[lines:, LANES:]
        high, low = split(jnp.concatenate([gr * fr - gi * fi, gr * fi + gi * fr], 1))
        c[r] = dot(jnp.concatenate([high, high, low], 1), back_ref[r])
    for row in range(0, lines, step):
        re = [c[r, row : row + step, :LANES] for r in range(RADIX)]
        im = [c[r, row : row + step, LANES:] for r in range(RADIX)]
        e0r, e0i, e1r, e1i = re[0] + re[2], im[0] + im[2], re[0] - re[2], im[0] - im[2]
        o0r, o0i, o1r, o1i = re[1] + re[3], im[1] + im[3], re[1] - re[3], im[1] - im[3]
        outs = (
            (e0r + o0r, e0i + o0i),
            (e1r - o1i, e1i + o1r),
            (e0r - o0r, e0i - o0i),
            (e1r + o1i, e1i - o1r),
        )
        for q, (dr, di) in enumerate(outs):
            at = slice(q * LANES, (q + 1) * LANES)
            ct, st = twist_ref[row : row + step, at], twist_ref[lines + row : lines + row + step, at]
            for part, value in enumerate((dr * ct - di * st, di * ct + dr * st)):
                high, low = split(value)
                rows = slice(part * lines + row, part * lines + row + step)
                dh[rows, at] = high
                dl[rows, at] = low
    for q in range(0, RADIX, 2):
        at = slice(q * LANES, (q + 2) * LANES)
        high = dh[:, at]
        y = dot(last_ref[...], jnp.concatenate([high, high, dl[:, at]], 0))
        y_ref[pl.ds(q, lines, stride=RADIX), :] = y[:, :LANES]
        y_ref[pl.ds(q + 1, lines, stride=RADIX), :] = y[:, LANES:]


def mix_kernel(query_ref, key_ref, value_ref, skip_ref, y_ref, out_ref):
    channels, width = query_ref.shape
    blocks = width // LANES
    skip = skip_ref[...]
    for q in range(blocks):
        at = pl.ds(q * LANES, LANES)
        y = y_ref[pl.ds(q, channels, stride=blocks), :]
        out_ref[:, at] = query_ref[:, at] * (y + skip * (key_ref[:, at] * value_ref[:, at]))


def convolve(x, lines, width):
    return pl.pallas_call(
        convolve_kernel,
        out_shape=jax.ShapeDtypeStruct((lines * RADIX, LANES), jnp.float32),
        scratch_shapes=[
            pltpu.VMEM((3 * lines, 2 * width), jnp.bfloat16),
            pltpu.VMEM((2 * lines, 2 * width), jnp.float32),
            pltpu.VMEM((RADIX, 2 * lines, 2 * LANES), jnp.bfloat16),
            pltpu.VMEM((RADIX, 2 * lines, 2 * LANES), jnp.bfloat16),
            pltpu.VMEM((RADIX, lines, 2 * LANES), jnp.float32),
            pltpu.VMEM((2 * lines, width), jnp.bfloat16),
            pltpu.VMEM((2 * lines, width), jnp.bfloat16),
        ],
        compiler_params=PARAMS,
    )(x, *tables(lines, width))


def body(query, key_branch, value_branch, long_filter, skip_gain):
    channels, width = query.shape
    lines = lax.axis_size("grp") * lax.axis_size("pos")
    blocks = width // LANES
    both = pl.pallas_call(
        gate_kernel,
        out_shape=jax.ShapeDtypeStruct((channels * 2 * blocks, LANES), jnp.float32),
        compiler_params=PARAMS,
    )(key_branch, value_branch, long_filter)
    both = lax.all_to_all(
        both.reshape(channels, 2 * blocks, LANES), AXES, split_axis=0, concat_axis=0, tiled=True
    )
    y = convolve(both.reshape(lines * 2 * blocks, LANES), lines, width)
    y = lax.all_to_all(y.reshape(lines, blocks, LANES), AXES, split_axis=0, concat_axis=0, tiled=True)
    return pl.pallas_call(
        mix_kernel,
        out_shape=jax.ShapeDtypeStruct((channels, width), jnp.float32),
        compiler_params=PARAMS,
    )(query, key_branch, value_branch, skip_gain.reshape(channels, 1), y.reshape(channels * blocks, LANES))


def solution(mesh):
    return jax.shard_map(
        body,
        mesh=mesh,
        in_specs=(P(None, AXES), P(None, AXES), P(None, AXES), P(None, AXES), P()),
        out_specs=P(None, AXES),
        check_vma=False,
    )
```

```python
import functools

import ml_dtypes
import numpy as np

import jax
import jax.numpy as jnp
from jax import lax
from jax.experimental import pallas as pl
from jax.experimental.pallas import tpu as pltpu
from jax.sharding import PartitionSpec as P

AXES = ("grp", "pos")
LANES = 128
RADIX = 4
CHUNKS = 2
ROW_PARTS = 1


def params(mib):
    return pltpu.CompilerParams(vmem_limit_bytes=mib * 2**20)


def turns(numerator, denominator):
    angle = 2.0 * np.pi * (numerator % denominator) / denominator
    return np.cos(angle), np.sin(angle)


def high_low(table):
    high = table.astype(ml_dtypes.bfloat16)
    low = (table - high.astype(np.float64)).astype(ml_dtypes.bfloat16)
    return high, low


def table_pair(table, axis):
    return np.concatenate(high_low(table), axis)


@functools.lru_cache
def tables(lines, width):
    length = lines * width
    line = np.arange(lines)
    offset = np.arange(width)
    c1, s1 = turns(np.outer(4 * line + 1, line), 4 * lines)
    ct, st = turns(np.outer(4 * line + 1, offset), 4 * length)
    small = np.arange(width // RADIX)
    forth, back = [], []
    for r in range(RADIX):
        c2, s2 = turns(np.outer(small, RADIX * small + r), width)
        block = np.block([[c2, -s2], [s2, c2]])
        forth.append(block)
        back.append(block.T / length)
    spread = np.concatenate([c1.reshape(ROW_PARTS, -1, lines), -s1.reshape(ROW_PARTS, -1, lines)], 1)
    return (
        table_pair(spread, -1),
        np.concatenate([ct, st], 0).astype(np.float32),
        table_pair(np.stack(forth), -2),
        table_pair(np.stack(back), -2),
        table_pair(np.concatenate([c1.T, -s1.T], 1), -1),
    )


def split(x):
    high = x.astype(jnp.bfloat16)
    return high, (x - high.astype(jnp.float32)).astype(jnp.bfloat16)


def dot(a, b):
    return jnp.dot(a, b, preferred_element_type=jnp.float32)


def dot_left(table, high, low):
    depth = high.shape[0]
    table = jnp.concatenate([table, table[:, :depth]], 1)
    return dot(table, jnp.concatenate([high, high, low], 0))


def dot_right(high, low, table):
    depth = high.shape[1]
    table = jnp.concatenate([table, table[:depth]], 0)
    return dot(jnp.concatenate([high, high, low], 1), table)


def gate_kernel(key_hbm, value_hbm, filter_hbm, skip_hbm, out_ref, key_ref, value_ref, filter_ref, skip_ref, sems):
    channels, width = key_ref.shape
    blocks = width // LANES
    part = channels // CHUNKS

    def copies(i):
        rows = pl.ds(i * part, part)
        pairs = ((key_hbm, key_ref), (value_hbm, value_ref), (filter_hbm, filter_ref))
        return [
            pltpu.make_async_copy(there.at[rows], here.at[rows], sems.at[n, i]) for n, (there, here) in enumerate(pairs)
        ]

    skip_copy = pltpu.make_async_copy(skip_hbm, skip_ref, sems.at[3, 0])
    skip_copy.start()
    for i in range(CHUNKS):
        for copy in copies(i):
            copy.start()
    first_device = (lax.axis_index(AXES[0]) == 0) & (lax.axis_index(AXES[1]) == 0)
    lane = lax.broadcasted_iota(jnp.int32, (part, LANES), 1)
    first_position = (lane == 0) & first_device
    skip_copy.wait()
    for i in range(CHUNKS):
        for copy in copies(i):
            copy.wait()
        rows = pl.ds(i * part, part)
        skip = jnp.broadcast_to(skip_ref[:, i * part : (i + 1) * part], (LANES, part)).T
        skip = jnp.where(first_position, skip, 0.0)
        for q in range(blocks):
            at = pl.ds(q * LANES, LANES)
            first = i * part * 2 * blocks + q
            lags = filter_ref[rows, at]
            out_ref[pl.ds(first, part, stride=2 * blocks), :] = key_ref[rows, at] * value_ref[rows, at]
            out_ref[pl.ds(first + blocks, part, stride=2 * blocks), :] = lags + skip if q == 0 else lags


def four(pairs, sign):
    (ar, ai), (br, bi), (cr, ci), (dr, di) = pairs
    e0r, e0i, e1r, e1i = ar + cr, ai + ci, ar - cr, ai - ci
    o0r, o0i, o1r, o1i = br + dr, bi + di, br - dr, bi - di
    turned, other = (e1r - o1i, e1i + o1r), (e1r + o1i, e1i - o1r)
    if sign < 0:
        turned, other = other, turned
    return (e0r + o0r, e0i + o0i), turned, (e0r - o0r, e0i - o0i), other


def convolve_kernel(x_ref, first_ref, twist_ref, forth_ref, back_ref, last_ref, y_ref, xh, xl, zh, zl, dh, dl):
    lines = y_ref.shape[0] // RADIX
    width = RADIX * LANES
    count = first_ref.shape[0]
    rows = lines // count
    for j in range(2 * RADIX):
        high, low = split(x_ref[pl.ds(j, lines, stride=2 * RADIX), :])
        at = pl.ds(j * LANES, LANES)
        xh[:, at] = high
        xl[:, at] = low
    for i in range(count):
        here, there = slice(i * rows, (i + 1) * rows), slice(lines + i * rows, lines + (i + 1) * rows)
        twist = [
            (twist_ref[here, q * LANES : (q + 1) * LANES], twist_ref[there, q * LANES : (q + 1) * LANES])
            for q in range(RADIX)
        ]
        for signal in range(2):
            at = slice(signal * width, (signal + 1) * width)
            spread = dot_left(first_ref[i], xh[:, at], xl[:, at])
            pairs = []
            for q, (ct, st) in enumerate(twist):
                at = slice(q * LANES, (q + 1) * LANES)
                re, im = spread[:rows, at], spread[rows:, at]
                pairs.append((re * ct + im * st, im * ct - re * st))
            at = slice(signal * rows, (signal + 1) * rows)
            for r, pair in enumerate(four(pairs, -1)):
                for part, value in enumerate(pair):
                    high, low = split(value)
                    zh[i, r, at, part * LANES : (part + 1) * LANES] = high
                    zl[i, r, at, part * LANES : (part + 1) * LANES] = low
        pairs = []
        for r in range(RADIX):
            spectra = dot_right(zh[i, r], zl[i, r], forth_ref[r])
            gr, gi = spectra[:rows, :LANES], spectra[:rows, LANES:]
            fr, fi = spectra[rows:, :LANES], spectra[rows:, LANES:]
            high, low = split(jnp.concatenate([gr * fr - gi * fi, gr * fi + gi * fr], 1))
            back = dot_right(high, low, back_ref[r])
            pairs.append((back[:, :LANES], back[:, LANES:]))
        for q, (re, im) in enumerate(four(pairs, 1)):
            ct, st = twist[q]
            at = slice(q * LANES, (q + 1) * LANES)
            dh[here, at], dl[here, at] = split(re * ct - im * st)
            dh[there, at], dl[there, at] = split(im * ct + re * st)
    for q in range(0, RADIX, 2):
        at = slice(q * LANES, (q + 2) * LANES)
        y = dot_left(last_ref[...], dh[:, at], dl[:, at])
        y_ref[pl.ds(q, lines, stride=RADIX), :] = y[:, :LANES]
        y_ref[pl.ds(q + 1, lines, stride=RADIX), :] = y[:, LANES:]


def mix_kernel(query_ref, y_ref, out_hbm, out_ref, sems):
    channels, width = query_ref.shape
    blocks = width // LANES
    part = channels // CHUNKS
    copies = []
    for i in range(CHUNKS):
        rows = pl.ds(i * part, part)
        for q in range(blocks):
            at = pl.ds(q * LANES, LANES)
            out_ref[rows, at] = query_ref[rows, at] * y_ref[pl.ds(i * part * blocks + q, part, stride=blocks), :]
        copies.append(pltpu.make_async_copy(out_ref.at[rows], out_hbm.at[rows], sems.at[i]))
        copies[-1].start()
    for copy in copies:
        copy.wait()


def convolve(x, lines, width):
    return pl.pallas_call(
        convolve_kernel,
        out_shape=jax.ShapeDtypeStruct((lines * RADIX, LANES), jnp.float32),
        scratch_shapes=[
            pltpu.VMEM((lines, 2 * width), jnp.bfloat16),
            pltpu.VMEM((lines, 2 * width), jnp.bfloat16),
            pltpu.VMEM((ROW_PARTS, RADIX, 2 * lines // ROW_PARTS, 2 * LANES), jnp.bfloat16),
            pltpu.VMEM((ROW_PARTS, RADIX, 2 * lines // ROW_PARTS, 2 * LANES), jnp.bfloat16),
            pltpu.VMEM((2 * lines, width), jnp.bfloat16),
            pltpu.VMEM((2 * lines, width), jnp.bfloat16),
        ],
        compiler_params=params(32),
    )(x, *tables(lines, width))


def body(query, key_branch, value_branch, long_filter, skip_gain):
    channels, width = query.shape
    lines = lax.axis_size("grp") * lax.axis_size("pos")
    blocks = width // LANES
    sources = [
        pltpu.with_memory_space_constraint(x, pltpu.HBM)
        for x in (key_branch, value_branch, long_filter, skip_gain.reshape(1, channels))
    ]
    both = pl.pallas_call(
        gate_kernel,
        out_shape=pltpu.VMEM((channels * 2 * blocks, LANES), jnp.float32),
        in_specs=[pl.BlockSpec(memory_space=pltpu.HBM)] * 4,
        scratch_shapes=[
            pltpu.VMEM((channels, width), jnp.float32),
            pltpu.VMEM((channels, width), jnp.float32),
            pltpu.VMEM((channels, width), jnp.float32),
            pltpu.VMEM((1, channels), jnp.float32),
            pltpu.SemaphoreType.DMA((4, CHUNKS)),
        ],
        compiler_params=params(16),
    )(*sources)
    both = lax.all_to_all(
        both.reshape(channels, 2 * blocks, LANES), AXES, split_axis=0, concat_axis=0, tiled=True
    )
    y = convolve(both.reshape(lines * 2 * blocks, LANES), lines, width)
    y = lax.all_to_all(y.reshape(lines, blocks, LANES), AXES, split_axis=0, concat_axis=0, tiled=True)
    return pl.pallas_call(
        mix_kernel,
        out_shape=jax.ShapeDtypeStruct((channels, width), jnp.float32),
        out_specs=pl.BlockSpec(memory_space=pltpu.HBM),
        scratch_shapes=[pltpu.VMEM((channels, width), jnp.float32), pltpu.SemaphoreType.DMA((CHUNKS,))],
        compiler_params=params(16),
    )(query, y.reshape(channels * blocks, LANES))


def solution(mesh):
    return jax.shard_map(
        body,
        mesh=mesh,
        in_specs=(P(None, AXES), P(None, AXES), P(None, AXES), P(None, AXES), P()),
        out_specs=P(None, AXES),
        check_vma=False,
    )
```

```python
import functools

import ml_dtypes
import numpy as np

import jax
import jax.numpy as jnp
from jax import lax
from jax.experimental import pallas as pl
from jax.experimental.pallas import tpu as pltpu
from jax.sharding import PartitionSpec as P

AXES = ("grp", "pos")
LANES = 128
RADIX = 4
CHUNKS = 2
STEP = 32


def params(mib):
    return pltpu.CompilerParams(vmem_limit_bytes=mib * 2**20)


def turns(numerator, denominator):
    angle = 2.0 * np.pi * (numerator % denominator) / denominator
    return np.cos(angle), np.sin(angle)


def high_low(table):
    high = table.astype(ml_dtypes.bfloat16)
    low = (table - high.astype(np.float64)).astype(ml_dtypes.bfloat16)
    return high, low


def table_pair(table, axis):
    return np.concatenate(high_low(table), axis)


@functools.lru_cache
def tables(lines, width):
    length = lines * width
    line = np.arange(lines)
    offset = np.arange(width)
    c1, s1 = turns(np.outer(4 * line + 1, line), 4 * lines)
    ct, st = turns(np.outer(4 * line + 1, offset), 4 * length)
    small = np.arange(width // RADIX)
    forth, back = [], []
    for r in range(RADIX):
        c2, s2 = turns(np.outer(small, RADIX * small + r), width)
        block = np.block([[c2, -s2], [s2, c2]])
        forth.append(block)
        back.append(block.T / length)
    return (
        table_pair(np.concatenate([c1, -s1], 0), -1),
        np.concatenate([ct, st], 0).astype(np.float32),
        table_pair(np.stack(forth), -2),
        table_pair(np.stack(back), -2),
        table_pair(np.concatenate([c1.T, -s1.T], 1), -1),
    )


def split(x):
    high = x.astype(jnp.bfloat16)
    return high, (x - high.astype(jnp.float32)).astype(jnp.bfloat16)


def dot(a, b):
    return jnp.dot(a, b, preferred_element_type=jnp.float32)


def dot_left(table, high, low):
    depth = high.shape[0]
    table = jnp.concatenate([table, table[:, :depth]], 1)
    return dot(table, jnp.concatenate([high, high, low], 0))


def dot_right(high, low, table):
    depth = high.shape[1]
    table = jnp.concatenate([table, table[:depth]], 0)
    return dot(jnp.concatenate([high, high, low], 1), table)


def gate_kernel(key_hbm, value_hbm, filter_hbm, skip_hbm, out_ref, key_ref, value_ref, filter_ref, skip_ref, sems):
    channels, width = key_ref.shape
    blocks = width // LANES
    part = channels // CHUNKS

    def copies(i):
        rows = pl.ds(i * part, part)
        pairs = ((key_hbm, key_ref), (value_hbm, value_ref), (filter_hbm, filter_ref))
        return [
            pltpu.make_async_copy(there.at[rows], here.at[rows], sems.at[n, i]) for n, (there, here) in enumerate(pairs)
        ]

    skip_copy = pltpu.make_async_copy(skip_hbm, skip_ref, sems.at[3, 0])
    skip_copy.start()
    for i in range(CHUNKS):
        for copy in copies(i):
            copy.start()
    first_device = (lax.axis_index(AXES[0]) == 0) & (lax.axis_index(AXES[1]) == 0)
    lane = lax.broadcasted_iota(jnp.int32, (part, LANES), 1)
    first_position = (lane == 0) & first_device
    skip_copy.wait()
    for i in range(CHUNKS):
        for copy in copies(i):
            copy.wait()
        rows = pl.ds(i * part, part)
        skip = jnp.broadcast_to(skip_ref[:, i * part : (i + 1) * part], (LANES, part)).T
        skip = jnp.where(first_position, skip, 0.0)
        for q in range(blocks):
            at = pl.ds(q * LANES, LANES)
            first = i * part * 2 * blocks + q
            lags = filter_ref[rows, at]
            out_ref[pl.ds(first, part, stride=2 * blocks), :] = key_ref[rows, at] * value_ref[rows, at]
            out_ref[pl.ds(first + blocks, part, stride=2 * blocks), :] = lags + skip if q == 0 else lags


def four(pairs, sign):
    (ar, ai), (br, bi), (cr, ci), (dr, di) = pairs
    e0r, e0i, e1r, e1i = ar + cr, ai + ci, ar - cr, ai - ci
    o0r, o0i, o1r, o1i = br + dr, bi + di, br - dr, bi - di
    turned, other = (e1r - o1i, e1i + o1r), (e1r + o1i, e1i - o1r)
    if sign < 0:
        turned, other = other, turned
    return (e0r + o0r, e0i + o0i), turned, (e0r - o0r, e0i - o0i), other


def convolve_kernel(x_ref, first_ref, twist_ref, forth_ref, back_ref, last_ref, y_ref, xh, xl, zh, zl, dh, dl):
    lines = y_ref.shape[0] // RADIX
    width = RADIX * LANES
    lower, upper = slice(0, lines), slice(lines, 2 * lines)

    def lanes(q):
        return slice(q * LANES, (q + 1) * LANES)

    def take(signal):
        for q in range(RADIX):
            j = signal * RADIX + q
            xh[:, lanes(j)], xl[:, lanes(j)] = split(x_ref[pl.ds(j, lines, stride=2 * RADIX), :])

    def over_lines(signal):
        at = slice(signal * width, (signal + 1) * width)
        return dot_left(first_ref[...], xh[:, at], xl[:, at])

    def turn(signal, spread):
        at = slice(signal * lines, (signal + 1) * lines)
        for row in range(0, lines, STEP):
            rows = slice(row, row + STEP)
            below = slice(lines + row, lines + row + STEP)
            here = slice(signal * lines + row, signal * lines + row + STEP)
            pairs = []
            for q in range(RADIX):
                re, im = spread[rows, lanes(q)], spread[below, lanes(q)]
                ct, st = twist_ref[rows, lanes(q)], twist_ref[below, lanes(q)]
                pairs.append((re * ct + im * st, im * ct - re * st))
            for r, pair in enumerate(four(pairs, -1)):
                for part, value in enumerate(pair):
                    zh[r, here, lanes(part)], zl[r, here, lanes(part)] = split(value)

    def over_offsets(signal, r):
        at = slice(signal * lines, (signal + 1) * lines)
        return dot_right(zh[r, at], zl[r, at], forth_ref[r])

    def product(g, f):
        gr, gi, fr, fi = g[:, :LANES], g[:, LANES:], f[:, :LANES], f[:, LANES:]
        return split(jnp.concatenate([gr * fr - gi * fi, gr * fi + gi * fr], 1))

    def turn_back(backs):
        for row in range(0, lines, STEP):
            rows = slice(row, row + STEP)
            below = slice(lines + row, lines + row + STEP)
            pairs = [(back[rows, :LANES], back[rows, LANES:]) for back in backs]
            for q, (re, im) in enumerate(four(pairs, 1)):
                ct, st = twist_ref[rows, lanes(q)], twist_ref[below, lanes(q)]
                dh[rows, lanes(q)], dl[rows, lanes(q)] = split(re * ct - im * st)
                dh[below, lanes(q)], dl[below, lanes(q)] = split(im * ct + re * st)

    take(0)
    spread_g = over_lines(0)
    take(1)
    spread_f = over_lines(1)
    turn(0, spread_g)
    gs = [over_offsets(0, r) for r in range(RADIX)]
    turn(1, spread_f)
    fs = [over_offsets(1, r) for r in range(RADIX)]
    backs = []
    for r in range(RADIX):
        high, low = product(gs[r], fs[r])
        backs.append(dot_right(high, low, back_ref[r]))
    turn_back(backs)
    for q in range(0, RADIX, 2):
        at = slice(q * LANES, (q + 2) * LANES)
        y = dot_left(last_ref[...], dh[:, at], dl[:, at])
        y_ref[pl.ds(q, lines, stride=RADIX), :] = y[:, :LANES]
        y_ref[pl.ds(q + 1, lines, stride=RADIX), :] = y[:, LANES:]


def mix_kernel(query_ref, y_ref, out_hbm, out_ref, sems):
    channels, width = query_ref.shape
    blocks = width // LANES
    part = channels // CHUNKS
    copies = []
    for i in range(CHUNKS):
        rows = pl.ds(i * part, part)
        for q in range(blocks):
            at = pl.ds(q * LANES, LANES)
            out_ref[rows, at] = query_ref[rows, at] * y_ref[pl.ds(i * part * blocks + q, part, stride=blocks), :]
        copies.append(pltpu.make_async_copy(out_ref.at[rows], out_hbm.at[rows], sems.at[i]))
        copies[-1].start()
    for copy in copies:
        copy.wait()


def convolve(x, lines, width):
    return pl.pallas_call(
        convolve_kernel,
        out_shape=jax.ShapeDtypeStruct((lines * RADIX, LANES), jnp.float32),
        scratch_shapes=[
            pltpu.VMEM((lines, 2 * width), jnp.bfloat16),
            pltpu.VMEM((lines, 2 * width), jnp.bfloat16),
            pltpu.VMEM((RADIX, 2 * lines, 2 * LANES), jnp.bfloat16),
            pltpu.VMEM((RADIX, 2 * lines, 2 * LANES), jnp.bfloat16),
            pltpu.VMEM((2 * lines, width), jnp.bfloat16),
            pltpu.VMEM((2 * lines, width), jnp.bfloat16),
        ],
        compiler_params=params(32),
    )(x, *tables(lines, width))


def body(query, key_branch, value_branch, long_filter, skip_gain):
    channels, width = query.shape
    lines = lax.axis_size("grp") * lax.axis_size("pos")
    blocks = width // LANES
    sources = [
        pltpu.with_memory_space_constraint(x, pltpu.HBM)
        for x in (key_branch, value_branch, long_filter, skip_gain.reshape(1, channels))
    ]
    both = pl.pallas_call(
        gate_kernel,
        out_shape=pltpu.VMEM((channels * 2 * blocks, LANES), jnp.float32),
        in_specs=[pl.BlockSpec(memory_space=pltpu.HBM)] * 4,
        scratch_shapes=[
            pltpu.VMEM((channels, width), jnp.float32),
            pltpu.VMEM((channels, width), jnp.float32),
            pltpu.VMEM((channels, width), jnp.float32),
            pltpu.VMEM((1, channels), jnp.float32),
            pltpu.SemaphoreType.DMA((4, CHUNKS)),
        ],
        compiler_params=params(16),
    )(*sources)
    both = lax.all_to_all(
        both.reshape(channels, 2 * blocks, LANES), AXES, split_axis=0, concat_axis=0, tiled=True
    )
    y = convolve(both.reshape(lines * 2 * blocks, LANES), lines, width)
    y = lax.all_to_all(y.reshape(lines, blocks, LANES), AXES, split_axis=0, concat_axis=0, tiled=True)
    return pl.pallas_call(
        mix_kernel,
        out_shape=jax.ShapeDtypeStruct((channels, width), jnp.float32),
        out_specs=pl.BlockSpec(memory_space=pltpu.HBM),
        scratch_shapes=[pltpu.VMEM((channels, width), jnp.float32), pltpu.SemaphoreType.DMA((CHUNKS,))],
        compiler_params=params(16),
    )(query, y.reshape(channels * blocks, LANES))


def solution(mesh):
    return jax.shard_map(
        body,
        mesh=mesh,
        in_specs=(P(None, AXES), P(None, AXES), P(None, AXES), P(None, AXES), P()),
        out_specs=P(None, AXES),
        check_vma=False,
    )
```

```python
import functools

import ml_dtypes
import numpy as np

import jax
import jax.numpy as jnp
from jax import lax
from jax.experimental import pallas as pl
from jax.experimental.pallas import tpu as pltpu
from jax.sharding import PartitionSpec as P

AXES = ("grp", "pos")
LANES = 128
RADIX = 4
CHUNKS = 2
STEP = 32


def params(mib):
    return pltpu.CompilerParams(vmem_limit_bytes=mib * 2**20)


def turns(numerator, denominator):
    angle = 2.0 * np.pi * (numerator % denominator) / denominator
    return np.cos(angle), np.sin(angle)


def high_low(table):
    high = table.astype(ml_dtypes.bfloat16)
    low = (table - high.astype(np.float64)).astype(ml_dtypes.bfloat16)
    return high, low


def table_pair(table, axis):
    return np.concatenate(high_low(table), axis)


@functools.lru_cache
def tables(lines, width):
    length = lines * width
    line = np.arange(lines)
    offset = np.arange(width)
    c1, s1 = turns(np.outer(4 * line + 1, line), 4 * lines)
    ct, st = turns(np.outer(4 * line + 1, offset), 4 * length)
    small = np.arange(width // RADIX)
    forth, back = [], []
    for r in range(RADIX):
        c2, s2 = turns(np.outer(small, RADIX * small + r), width)
        block = np.block([[c2, -s2], [s2, c2]])
        forth.append(block)
        back.append(block.T / length)
    return (
        table_pair(np.concatenate([c1, -s1], 0), -1),
        np.concatenate([ct, st], 0).astype(np.float32),
        table_pair(np.stack(forth), -2),
        table_pair(np.stack(back), -2),
        table_pair(np.concatenate([c1.T, -s1.T], 1), -1),
    )


def split(x):
    high = x.astype(jnp.bfloat16)
    return high, (x - high.astype(jnp.float32)).astype(jnp.bfloat16)


def dot(a, b):
    return jnp.dot(a, b, preferred_element_type=jnp.float32)


def dot_left(table, high, low):
    depth = high.shape[0]
    table = jnp.concatenate([table, table[:, :depth]], 1)
    return dot(table, jnp.concatenate([high, high, low], 0))


def dot_right(high, low, table):
    depth = high.shape[1]
    table = jnp.concatenate([table, table[:depth]], 0)
    return dot(jnp.concatenate([high, high, low], 1), table)


def gate_kernel(key_hbm, value_hbm, filter_hbm, skip_hbm, out_ref, key_ref, value_ref, skip_ref, sems, filter_sems, skip_sem):
    channels, width = key_ref.shape
    blocks = width // LANES
    part = channels // CHUNKS
    flat = out_ref.reshape(channels * 2 * blocks, LANES)

    def copies(i):
        rows = pl.ds(i * part, part)
        pairs = ((key_hbm, key_ref), (value_hbm, value_ref))
        return [
            pltpu.make_async_copy(there.at[rows], here.at[rows], sems.at[n, i]) for n, (there, here) in enumerate(pairs)
        ]

    for i in range(CHUNKS):
        for copy in copies(i):
            copy.start()
    filter_copies = [
        pltpu.make_async_copy(
            filter_hbm.at[:, pl.ds(q * LANES, LANES)], out_ref.at[:, blocks + q, :], filter_sems.at[q]
        )
        for q in range(blocks)
    ]
    for copy in filter_copies:
        copy.start()
    skip_copy = pltpu.make_async_copy(skip_hbm, skip_ref, skip_sem)
    skip_copy.start()
    for i in range(CHUNKS):
        for copy in copies(i):
            copy.wait()
        rows = pl.ds(i * part, part)
        for q in range(blocks):
            at = pl.ds(q * LANES, LANES)
            flat[pl.ds(i * part * 2 * blocks + q, part, stride=2 * blocks), :] = key_ref[rows, at] * value_ref[rows, at]
    skip_copy.wait()
    for copy in filter_copies:
        copy.wait()

    @pl.when((lax.axis_index(AXES[0]) == 0) & (lax.axis_index(AXES[1]) == 0))
    def _():
        lane = lax.broadcasted_iota(jnp.int32, (channels, LANES), 1)
        skip = jnp.broadcast_to(skip_ref[...], (LANES, channels)).T
        at = pl.ds(blocks, channels, stride=2 * blocks)
        flat[at, :] = flat[at, :] + jnp.where(lane == 0, skip, 0.0)


def four(pairs, sign):
    (ar, ai), (br, bi), (cr, ci), (dr, di) = pairs
    e0r, e0i, e1r, e1i = ar + cr, ai + ci, ar - cr, ai - ci
    o0r, o0i, o1r, o1i = br + dr, bi + di, br - dr, bi - di
    turned, other = (e1r - o1i, e1i + o1r), (e1r + o1i, e1i - o1r)
    if sign < 0:
        turned, other = other, turned
    return (e0r + o0r, e0i + o0i), turned, (e0r - o0r, e0i - o0i), other


def convolve_kernel(x_ref, first_ref, twist_ref, forth_ref, back_ref, last_ref, y_ref, xh, xl, zh, zl, dh, dl):
    lines = y_ref.shape[0] // RADIX
    width = RADIX * LANES
    lower, upper = slice(0, lines), slice(lines, 2 * lines)

    def lanes(q):
        return slice(q * LANES, (q + 1) * LANES)

    def take(signal):
        for q in range(RADIX):
            j = signal * RADIX + q
            xh[:, lanes(j)], xl[:, lanes(j)] = split(x_ref[pl.ds(j, lines, stride=2 * RADIX), :])

    def over_lines(signal):
        at = slice(signal * width, (signal + 1) * width)
        return dot_left(first_ref[...], xh[:, at], xl[:, at])

    def turn(signal, spread):
        at = slice(signal * lines, (signal + 1) * lines)
        for row in range(0, lines, STEP):
            rows = slice(row, row + STEP)
            below = slice(lines + row, lines + row + STEP)
            here = slice(signal * lines + row, signal * lines + row + STEP)
            pairs = []
            for q in range(RADIX):
                re, im = spread[rows, lanes(q)], spread[below, lanes(q)]
                ct, st = twist_ref[rows, lanes(q)], twist_ref[below, lanes(q)]
                pairs.append((re * ct + im * st, im * ct - re * st))
            for r, pair in enumerate(four(pairs, -1)):
                for part, value in enumerate(pair):
                    zh[r, here, lanes(part)], zl[r, here, lanes(part)] = split(value)

    def over_offsets(signal, r):
        at = slice(signal * lines, (signal + 1) * lines)
        return dot_right(zh[r, at], zl[r, at], forth_ref[r])

    def product(g, f):
        gr, gi, fr, fi = g[:, :LANES], g[:, LANES:], f[:, :LANES], f[:, LANES:]
        return split(jnp.concatenate([gr * fr - gi * fi, gr * fi + gi * fr], 1))

    def turn_back(backs):
        for row in range(0, lines, STEP):
            rows = slice(row, row + STEP)
            below = slice(lines + row, lines + row + STEP)
            pairs = [(back[rows, :LANES], back[rows, LANES:]) for back in backs]
            for q, (re, im) in enumerate(four(pairs, 1)):
                ct, st = twist_ref[rows, lanes(q)], twist_ref[below, lanes(q)]
                dh[rows, lanes(q)], dl[rows, lanes(q)] = split(re * ct - im * st)
                dh[below, lanes(q)], dl[below, lanes(q)] = split(im * ct + re * st)

    take(0)
    spread_g = over_lines(0)
    take(1)
    spread_f = over_lines(1)
    turn(0, spread_g)
    gs = [over_offsets(0, r) for r in range(RADIX)]
    turn(1, spread_f)
    fs = [over_offsets(1, r) for r in range(RADIX)]
    backs = []
    for r in range(RADIX):
        high, low = product(gs[r], fs[r])
        backs.append(dot_right(high, low, back_ref[r]))
    turn_back(backs)
    for q in range(0, RADIX, 2):
        at = slice(q * LANES, (q + 2) * LANES)
        y = dot_left(last_ref[...], dh[:, at], dl[:, at])
        y_ref[pl.ds(q, lines, stride=RADIX), :] = y[:, :LANES]
        y_ref[pl.ds(q + 1, lines, stride=RADIX), :] = y[:, LANES:]


def mix_kernel(query_ref, y_ref, out_hbm, out_ref, sems):
    channels, width = query_ref.shape
    blocks = width // LANES
    part = channels // CHUNKS
    copies = []
    for i in range(CHUNKS):
        rows = pl.ds(i * part, part)
        for q in range(blocks):
            at = pl.ds(q * LANES, LANES)
            out_ref[rows, at] = query_ref[rows, at] * y_ref[pl.ds(i * part * blocks + q, part, stride=blocks), :]
        copies.append(pltpu.make_async_copy(out_ref.at[rows], out_hbm.at[rows], sems.at[i]))
        copies[-1].start()
    for copy in copies:
        copy.wait()


def convolve(x, lines, width):
    return pl.pallas_call(
        convolve_kernel,
        out_shape=jax.ShapeDtypeStruct((lines * RADIX, LANES), jnp.float32),
        scratch_shapes=[
            pltpu.VMEM((lines, 2 * width), jnp.bfloat16),
            pltpu.VMEM((lines, 2 * width), jnp.bfloat16),
            pltpu.VMEM((RADIX, 2 * lines, 2 * LANES), jnp.bfloat16),
            pltpu.VMEM((RADIX, 2 * lines, 2 * LANES), jnp.bfloat16),
            pltpu.VMEM((2 * lines, width), jnp.bfloat16),
            pltpu.VMEM((2 * lines, width), jnp.bfloat16),
        ],
        compiler_params=params(32),
    )(x, *tables(lines, width))


def body(query, key_branch, value_branch, long_filter, skip_gain):
    channels, width = query.shape
    lines = lax.axis_size("grp") * lax.axis_size("pos")
    blocks = width // LANES
    sources = [
        pltpu.with_memory_space_constraint(x, pltpu.HBM)
        for x in (key_branch, value_branch, long_filter, skip_gain.reshape(1, channels))
    ]
    both = pl.pallas_call(
        gate_kernel,
        out_shape=pltpu.VMEM((channels, 2 * blocks, LANES), jnp.float32),
        in_specs=[pl.BlockSpec(memory_space=pltpu.HBM)] * 4,
        scratch_shapes=[
            pltpu.VMEM((channels, width), jnp.float32),
            pltpu.VMEM((channels, width), jnp.float32),
            pltpu.VMEM((1, channels), jnp.float32),
            pltpu.SemaphoreType.DMA((2, CHUNKS)),
            pltpu.SemaphoreType.DMA((blocks,)),
            pltpu.SemaphoreType.DMA,
        ],
        compiler_params=params(16),
    )(*sources)
    both = lax.all_to_all(both, AXES, split_axis=0, concat_axis=0, tiled=True)
    y = convolve(both.reshape(lines * 2 * blocks, LANES), lines, width)
    y = lax.all_to_all(y.reshape(lines, blocks, LANES), AXES, split_axis=0, concat_axis=0, tiled=True)
    return pl.pallas_call(
        mix_kernel,
        out_shape=jax.ShapeDtypeStruct((channels, width), jnp.float32),
        out_specs=pl.BlockSpec(memory_space=pltpu.HBM),
        scratch_shapes=[pltpu.VMEM((channels, width), jnp.float32), pltpu.SemaphoreType.DMA((CHUNKS,))],
        compiler_params=params(16),
    )(query, y.reshape(channels * blocks, LANES))


def solution(mesh):
    return jax.shard_map(
        body,
        mesh=mesh,
        in_specs=(P(None, AXES), P(None, AXES), P(None, AXES), P(None, AXES), P()),
        out_specs=P(None, AXES),
        check_vma=False,
    )
```

```python
import functools

import ml_dtypes
import numpy as np

import jax
import jax.numpy as jnp
from jax import lax
from jax.experimental import pallas as pl
from jax.experimental.pallas import tpu as pltpu
from jax.sharding import PartitionSpec as P

AXES = ("grp", "pos")
LANES = 128
RADIX = 4
CHUNKS = 2
STEP = 32


def params(mib):
    return pltpu.CompilerParams(vmem_limit_bytes=mib * 2**20)


def turns(numerator, denominator):
    angle = 2.0 * np.pi * (numerator % denominator) / denominator
    return np.cos(angle), np.sin(angle)


def high_low(table):
    high = table.astype(ml_dtypes.bfloat16)
    low = (table - high.astype(np.float64)).astype(ml_dtypes.bfloat16)
    return high, low


def table_pair(table, axis):
    return np.concatenate(high_low(table), axis)


@functools.lru_cache
def tables(lines, width):
    length = lines * width
    line = np.arange(lines)
    offset = np.arange(width)
    half = line[: lines // 2]
    c1, s1 = turns(np.outer(4 * line + 1, line), 4 * lines)
    last = []
    for j in range(2):
        ch, sh = turns(np.outer(2 * half + j, 4 * half + 1), 4 * lines)
        last.append(table_pair(np.concatenate([ch, -sh], 1), -1))
    ct, st = turns(np.outer(4 * line + 1, offset), 4 * length)
    small = np.arange(width // RADIX)
    forth, back = [], []
    for r in range(RADIX):
        c2, s2 = turns(np.outer(small, RADIX * small + r), width)
        block = np.block([[c2, -s2], [s2, c2]])
        forth.append(block)
        back.append(block.T / length)
    return (
        table_pair(np.concatenate([c1, -s1], 0), -1),
        np.concatenate([ct, st], 0).astype(np.float32),
        table_pair(np.stack(forth), -2),
        table_pair(np.stack(back), -2),
        np.stack(last),
    )


def split(x):
    high = x.astype(jnp.bfloat16)
    return high, (x - high.astype(jnp.float32)).astype(jnp.bfloat16)


def dot(a, b):
    return jnp.dot(a, b, preferred_element_type=jnp.float32)


def dot_left(table, high, low):
    depth = high.shape[0]
    table = jnp.concatenate([table, table[:, :depth]], 1)
    return dot(table, jnp.concatenate([high, high, low], 0))


def dot_right(high, low, table):
    depth = high.shape[1]
    table = jnp.concatenate([table, table[:depth]], 0)
    return dot(jnp.concatenate([high, high, low], 1), table)


def gate_kernel(key_hbm, value_hbm, filter_hbm, skip_hbm, out_ref, key_ref, value_ref, skip_ref, sems, filter_sems, skip_sem):
    channels, width = key_ref.shape
    blocks = width // LANES
    part = channels // CHUNKS
    flat = out_ref.reshape(channels * 2 * blocks, LANES)

    def copies(i):
        rows = pl.ds(i * part, part)
        pairs = ((key_hbm, key_ref), (value_hbm, value_ref))
        return [
            pltpu.make_async_copy(there.at[rows], here.at[rows], sems.at[n, i]) for n, (there, here) in enumerate(pairs)
        ]

    for i in range(CHUNKS):
        for copy in copies(i):
            copy.start()
    filter_copies = [
        pltpu.make_async_copy(
            filter_hbm.at[:, pl.ds(q * LANES, LANES)], out_ref.at[:, blocks + q, :], filter_sems.at[q]
        )
        for q in range(blocks)
    ]
    for copy in filter_copies:
        copy.start()
    skip_copy = pltpu.make_async_copy(skip_hbm, skip_ref, skip_sem)
    skip_copy.start()
    for i in range(CHUNKS):
        for copy in copies(i):
            copy.wait()
        rows = pl.ds(i * part, part)
        for q in range(blocks):
            at = pl.ds(q * LANES, LANES)
            flat[pl.ds(i * part * 2 * blocks + q, part, stride=2 * blocks), :] = key_ref[rows, at] * value_ref[rows, at]
    skip_copy.wait()
    for copy in filter_copies:
        copy.wait()

    @pl.when((lax.axis_index(AXES[0]) == 0) & (lax.axis_index(AXES[1]) == 0))
    def _():
        lane = lax.broadcasted_iota(jnp.int32, (channels, LANES), 1)
        skip = jnp.broadcast_to(skip_ref[...], (LANES, channels)).T
        at = pl.ds(blocks, channels, stride=2 * blocks)
        flat[at, :] = flat[at, :] + jnp.where(lane == 0, skip, 0.0)


def four(pairs, sign):
    (ar, ai), (br, bi), (cr, ci), (dr, di) = pairs
    e0r, e0i, e1r, e1i = ar + cr, ai + ci, ar - cr, ai - ci
    o0r, o0i, o1r, o1i = br + dr, bi + di, br - dr, bi - di
    turned, other = (e1r - o1i, e1i + o1r), (e1r + o1i, e1i - o1r)
    if sign < 0:
        turned, other = other, turned
    return (e0r + o0r, e0i + o0i), turned, (e0r - o0r, e0i - o0i), other


def convolve_kernel(x_ref, first_ref, twist_ref, forth_ref, back_ref, last_ref, y_ref, xh, xl, zh, zl, dh, dl):
    lines = y_ref.shape[0] // RADIX
    width = RADIX * LANES
    half = lines // 2

    def lanes(q):
        return slice(q * LANES, (q + 1) * LANES)

    def take(signal):
        for q in range(RADIX):
            j = signal * RADIX + q
            xh[:, lanes(j)], xl[:, lanes(j)] = split(x_ref[pl.ds(j, lines, stride=2 * RADIX), :])

    def over_lines(signal):
        at = slice(signal * width, (signal + 1) * width)
        return dot_left(first_ref[...], xh[:, at], xl[:, at])

    def turn(signal, spread):
        at = slice(signal * lines, (signal + 1) * lines)
        for row in range(0, lines, STEP):
            rows = slice(row, row + STEP)
            below = slice(lines + row, lines + row + STEP)
            here = slice(signal * lines + row, signal * lines + row + STEP)
            pairs = []
            for q in range(RADIX):
                re, im = spread[rows, lanes(q)], spread[below, lanes(q)]
                ct, st = twist_ref[rows, lanes(q)], twist_ref[below, lanes(q)]
                pairs.append((re * ct + im * st, im * ct - re * st))
            for r, pair in enumerate(four(pairs, -1)):
                for part, value in enumerate(pair):
                    zh[r, here, lanes(part)], zl[r, here, lanes(part)] = split(value)

    def over_offsets(signal, r):
        at = slice(signal * lines, (signal + 1) * lines)
        return dot_right(zh[r, at], zl[r, at], forth_ref[r])

    def product(g, f):
        gr, gi, fr, fi = g[:, :LANES], g[:, LANES:], f[:, :LANES], f[:, LANES:]
        return split(jnp.concatenate([gr * fr - gi * fi, gr * fi + gi * fr], 1))

    def turned_back(backs, row):
        pairs = [(back[row : row + STEP, :LANES], back[row : row + STEP, LANES:]) for back in backs]
        turned = []
        for q, (re, im) in enumerate(four(pairs, 1)):
            ct = twist_ref[row : row + STEP, lanes(q)]
            st = twist_ref[lines + row : lines + row + STEP, lanes(q)]
            turned.append((re * ct - im * st, im * ct + re * st))
        return turned

    def turn_back(backs):
        for row in range(0, half, STEP):
            both = zip(turned_back(backs, row), turned_back(backs, half + row))
            for q, (near, far) in enumerate(both):
                for part in range(2):
                    at = slice(part * half + row, part * half + row + STEP)
                    dh[0, at, lanes(q)], dl[0, at, lanes(q)] = split(near[part] + far[part])
                    dh[1, at, lanes(q)], dl[1, at, lanes(q)] = split(near[part] - far[part])

    take(0)
    spread_g = over_lines(0)
    take(1)
    spread_f = over_lines(1)
    turn(0, spread_g)
    gs = [over_offsets(0, r) for r in range(RADIX)]
    turn(1, spread_f)
    fs = [over_offsets(1, r) for r in range(RADIX)]
    backs = []
    for r in range(RADIX):
        high, low = product(gs[r], fs[r])
        backs.append(dot_right(high, low, back_ref[r]))
    turn_back(backs)
    for j in range(2):
        y = dot_left(last_ref[j], dh[j], dl[j])
        for q in range(RADIX):
            y_ref[pl.ds(j * RADIX + q, half, stride=2 * RADIX), :] = y[:, lanes(q)]


def mix_kernel(query_ref, y_ref, out_hbm, out_ref, sems):
    channels, width = query_ref.shape
    blocks = width // LANES
    part = channels // CHUNKS
    copies = []
    for i in range(CHUNKS):
        rows = pl.ds(i * part, part)
        for q in range(blocks):
            at = pl.ds(q * LANES, LANES)
            out_ref[rows, at] = query_ref[rows, at] * y_ref[pl.ds(i * part * blocks + q, part, stride=blocks), :]
        copies.append(pltpu.make_async_copy(out_ref.at[rows], out_hbm.at[rows], sems.at[i]))
        copies[-1].start()
    for copy in copies:
        copy.wait()


def convolve(x, lines, width):
    return pl.pallas_call(
        convolve_kernel,
        out_shape=jax.ShapeDtypeStruct((lines * RADIX, LANES), jnp.float32),
        scratch_shapes=[
            pltpu.VMEM((lines, 2 * width), jnp.bfloat16),
            pltpu.VMEM((lines, 2 * width), jnp.bfloat16),
            pltpu.VMEM((RADIX, 2 * lines, 2 * LANES), jnp.bfloat16),
            pltpu.VMEM((RADIX, 2 * lines, 2 * LANES), jnp.bfloat16),
            pltpu.VMEM((2, lines, width), jnp.bfloat16),
            pltpu.VMEM((2, lines, width), jnp.bfloat16),
        ],
        compiler_params=params(32),
    )(x, *tables(lines, width))


def body(query, key_branch, value_branch, long_filter, skip_gain):
    channels, width = query.shape
    lines = lax.axis_size("grp") * lax.axis_size("pos")
    blocks = width // LANES
    sources = [
        pltpu.with_memory_space_constraint(x, pltpu.HBM)
        for x in (key_branch, value_branch, long_filter, skip_gain.reshape(1, channels))
    ]
    both = pl.pallas_call(
        gate_kernel,
        out_shape=pltpu.VMEM((channels, 2 * blocks, LANES), jnp.float32),
        in_specs=[pl.BlockSpec(memory_space=pltpu.HBM)] * 4,
        scratch_shapes=[
            pltpu.VMEM((channels, width), jnp.float32),
            pltpu.VMEM((channels, width), jnp.float32),
            pltpu.VMEM((1, channels), jnp.float32),
            pltpu.SemaphoreType.DMA((2, CHUNKS)),
            pltpu.SemaphoreType.DMA((blocks,)),
            pltpu.SemaphoreType.DMA,
        ],
        compiler_params=params(16),
    )(*sources)
    both = lax.all_to_all(both, AXES, split_axis=0, concat_axis=0, tiled=True)
    y = convolve(both.reshape(lines * 2 * blocks, LANES), lines, width)
    y = lax.all_to_all(y.reshape(lines, blocks, LANES), AXES, split_axis=0, concat_axis=0, tiled=True)
    return pl.pallas_call(
        mix_kernel,
        out_shape=jax.ShapeDtypeStruct((channels, width), jnp.float32),
        out_specs=pl.BlockSpec(memory_space=pltpu.HBM),
        scratch_shapes=[pltpu.VMEM((channels, width), jnp.float32), pltpu.SemaphoreType.DMA((CHUNKS,))],
        compiler_params=params(16),
    )(query, y.reshape(channels * blocks, LANES))


def solution(mesh):
    return jax.shard_map(
        body,
        mesh=mesh,
        in_specs=(P(None, AXES), P(None, AXES), P(None, AXES), P(None, AXES), P()),
        out_specs=P(None, AXES),
        check_vma=False,
    )
```

```python
import functools

import ml_dtypes
import numpy as np

import jax
import jax.numpy as jnp
from jax import lax
from jax.experimental import pallas as pl
from jax.experimental.pallas import tpu as pltpu
from jax.sharding import PartitionSpec as P

AXES = ("grp", "pos")
LANES = 128
RADIX = 4
CHUNKS = 2
STEP = 32


def params(mib):
    return pltpu.CompilerParams(vmem_limit_bytes=mib * 2**20)


def turns(numerator, denominator):
    angle = 2.0 * np.pi * (numerator % denominator) / denominator
    return np.cos(angle), np.sin(angle)


def high_low(table):
    high = table.astype(ml_dtypes.bfloat16)
    low = (table - high.astype(np.float64)).astype(ml_dtypes.bfloat16)
    return high, low


def table_pair(table, axis):
    return np.concatenate(high_low(table), axis)


@functools.lru_cache
def tables(lines, width):
    length = lines * width
    line = np.arange(lines)
    offset = np.arange(width)
    half = line[: lines // 2]
    first, last = [], []
    for j in range(2):
        ch, sh = turns(np.outer(4 * half + 1, 2 * half + j), 4 * lines)
        first.append(table_pair(np.concatenate([ch, -sh], 0), -1))
        ch, sh = turns(np.outer(2 * half + j, 4 * half + 1), 4 * lines)
        last.append(table_pair(np.concatenate([ch, -sh], 1), -1))
    ct, st = turns(np.outer(4 * line + 1, offset), 4 * length)
    small = np.arange(width // RADIX)
    forth, back = [], []
    for r in range(RADIX):
        c2, s2 = turns(np.outer(small, RADIX * small + r), width)
        block = np.block([[c2, -s2], [s2, c2]])
        forth.append(block)
        back.append(block.T / length)
    return (
        np.stack(first),
        np.concatenate([ct, st], 0).astype(np.float32),
        table_pair(np.stack(forth), -2),
        table_pair(np.stack(back), -2),
        np.stack(last),
    )


def split(x):
    high = x.astype(jnp.bfloat16)
    return high, (x - high.astype(jnp.float32)).astype(jnp.bfloat16)


def dot(a, b):
    return jnp.dot(a, b, preferred_element_type=jnp.float32)


def dot_left(table, high, low):
    depth = high.shape[0]
    table = jnp.concatenate([table, table[:, :depth]], 1)
    return dot(table, jnp.concatenate([high, high, low], 0))


def dot_right(high, low, table):
    depth = high.shape[1]
    table = jnp.concatenate([table, table[:depth]], 0)
    return dot(jnp.concatenate([high, high, low], 1), table)


def gate_kernel(key_hbm, value_hbm, filter_hbm, skip_hbm, out_ref, key_ref, value_ref, skip_ref, sems, filter_sems, skip_sem):
    channels, width = key_ref.shape
    blocks = width // LANES
    part = channels // CHUNKS
    flat = out_ref.reshape(channels * 2 * blocks, LANES)

    def copies(i):
        rows = pl.ds(i * part, part)
        pairs = ((key_hbm, key_ref), (value_hbm, value_ref))
        return [
            pltpu.make_async_copy(there.at[rows], here.at[rows], sems.at[n, i]) for n, (there, here) in enumerate(pairs)
        ]

    for i in range(CHUNKS):
        for copy in copies(i):
            copy.start()
    filter_copies = [
        pltpu.make_async_copy(
            filter_hbm.at[:, pl.ds(q * LANES, LANES)], out_ref.at[:, blocks + q, :], filter_sems.at[q]
        )
        for q in range(blocks)
    ]
    for copy in filter_copies:
        copy.start()
    skip_copy = pltpu.make_async_copy(skip_hbm, skip_ref, skip_sem)
    skip_copy.start()
    for i in range(CHUNKS):
        for copy in copies(i):
            copy.wait()
        rows = pl.ds(i * part, part)
        for q in range(blocks):
            at = pl.ds(q * LANES, LANES)
            flat[pl.ds(i * part * 2 * blocks + q, part, stride=2 * blocks), :] = key_ref[rows, at] * value_ref[rows, at]
    skip_copy.wait()
    for copy in filter_copies:
        copy.wait()

    @pl.when((lax.axis_index(AXES[0]) == 0) & (lax.axis_index(AXES[1]) == 0))
    def _():
        lane = lax.broadcasted_iota(jnp.int32, (channels, LANES), 1)
        skip = jnp.broadcast_to(skip_ref[...], (LANES, channels)).T
        at = pl.ds(blocks, channels, stride=2 * blocks)
        flat[at, :] = flat[at, :] + jnp.where(lane == 0, skip, 0.0)


def four(pairs, sign):
    (ar, ai), (br, bi), (cr, ci), (dr, di) = pairs
    e0r, e0i, e1r, e1i = ar + cr, ai + ci, ar - cr, ai - ci
    o0r, o0i, o1r, o1i = br + dr, bi + di, br - dr, bi - di
    turned, other = (e1r - o1i, e1i + o1r), (e1r + o1i, e1i - o1r)
    if sign < 0:
        turned, other = other, turned
    return (e0r + o0r, e0i + o0i), turned, (e0r - o0r, e0i - o0i), other


def convolve_kernel(x_ref, first_ref, twist_ref, forth_ref, back_ref, last_ref, y_ref, xh, xl, zh, zl, dh, dl):
    lines = y_ref.shape[0] // RADIX
    width = RADIX * LANES
    half = lines // 2

    def lanes(q):
        return slice(q * LANES, (q + 1) * LANES)

    def take(signal):
        for q in range(RADIX):
            n = signal * RADIX + q
            for j in range(2):
                at = slice(j * half, (j + 1) * half)
                xh[at, lanes(n)], xl[at, lanes(n)] = split(
                    x_ref[pl.ds(2 * RADIX * j + n, half, stride=4 * RADIX), :]
                )

    def over_lines(signal):
        at = slice(signal * width, (signal + 1) * width)
        spread = []
        for j in range(2):
            rows = slice(j * half, (j + 1) * half)
            spread.append(dot_left(first_ref[j], xh[rows, at], xl[rows, at]))
        return spread

    def turn(signal, spread):
        even, odd = spread
        for row in range(0, lines, STEP):
            here = slice(signal * lines + row, signal * lines + row + STEP)
            k = row % half
            pairs = []
            for q in range(RADIX):
                er, ei = even[k : k + STEP, lanes(q)], even[half + k : half + k + STEP, lanes(q)]
                fr, fi = odd[k : k + STEP, lanes(q)], odd[half + k : half + k + STEP, lanes(q)]
                re, im = (er + fr, ei + fi) if row < half else (er - fr, ei - fi)
                ct, st = twist_ref[row : row + STEP, lanes(q)], twist_ref[lines + row : lines + row + STEP, lanes(q)]
                pairs.append((re * ct + im * st, im * ct - re * st))
            for r, pair in enumerate(four(pairs, -1)):
                for part, value in enumerate(pair):
                    zh[r, here, lanes(part)], zl[r, here, lanes(part)] = split(value)

    def over_offsets(signal, r):
        at = slice(signal * lines, (signal + 1) * lines)
        return dot_right(zh[r, at], zl[r, at], forth_ref[r])

    def product(g, f):
        gr, gi, fr, fi = g[:, :LANES], g[:, LANES:], f[:, :LANES], f[:, LANES:]
        return split(jnp.concatenate([gr * fr - gi * fi, gr * fi + gi * fr], 1))

    def turned_back(backs, row):
        pairs = [(back[row : row + STEP, :LANES], back[row : row + STEP, LANES:]) for back in backs]
        turned = []
        for q, (re, im) in enumerate(four(pairs, 1)):
            ct = twist_ref[row : row + STEP, lanes(q)]
            st = twist_ref[lines + row : lines + row + STEP, lanes(q)]
            turned.append((re * ct - im * st, im * ct + re * st))
        return turned

    def turn_back(backs):
        later = []
        for row in range(0, half, STEP):
            both = zip(turned_back(backs, row), turned_back(backs, half + row))
            for q, (near, far) in enumerate(both):
                for part in range(2):
                    at = slice(part * half + row, part * half + row + STEP)
                    dh[0, at, lanes(q)], dl[0, at, lanes(q)] = split(near[part] + far[part])
                    later.append((at, lanes(q), near[part] - far[part]))
        return later

    take(0)
    spread_g = over_lines(0)
    take(1)
    spread_f = over_lines(1)
    turn(0, spread_g)
    gs = [over_offsets(0, r) for r in range(RADIX)]
    turn(1, spread_f)
    fs = [over_offsets(1, r) for r in range(RADIX)]
    backs = []
    for r in range(RADIX):
        parts = []
        for k in range(0, lines, half):
            rows = slice(k, k + half)
            high, low = product(gs[r][rows], fs[r][rows])
            parts.append(dot_right(high, low, back_ref[r]))
        backs.append(jnp.concatenate(parts, 0))
    later = turn_back(backs)
    for j in range(2):
        y = dot_left(last_ref[j], dh[j], dl[j])
        if j == 0:
            for rows, at, value in later:
                dh[1, rows, at], dl[1, rows, at] = split(value)
        for q in range(RADIX):
            y_ref[pl.ds(j * RADIX + q, half, stride=2 * RADIX), :] = y[:, lanes(q)]


def mix_kernel(query_ref, y_ref, out_hbm, out_ref, sems):
    channels, width = query_ref.shape
    blocks = width // LANES
    part = channels // CHUNKS
    copies = []
    for i in range(CHUNKS):
        rows = pl.ds(i * part, part)
        for q in range(blocks):
            at = pl.ds(q * LANES, LANES)
            out_ref[rows, at] = query_ref[rows, at] * y_ref[pl.ds(i * part * blocks + q, part, stride=blocks), :]
        copies.append(pltpu.make_async_copy(out_ref.at[rows], out_hbm.at[rows], sems.at[i]))
        copies[-1].start()
    for copy in copies:
        copy.wait()


def convolve(x, lines, width):
    return pl.pallas_call(
        convolve_kernel,
        out_shape=jax.ShapeDtypeStruct((lines * RADIX, LANES), jnp.float32),
        scratch_shapes=[
            pltpu.VMEM((lines, 2 * width), jnp.bfloat16),
            pltpu.VMEM((lines, 2 * width), jnp.bfloat16),
            pltpu.VMEM((RADIX, 2 * lines, 2 * LANES), jnp.bfloat16),
            pltpu.VMEM((RADIX, 2 * lines, 2 * LANES), jnp.bfloat16),
            pltpu.VMEM((2, lines, width), jnp.bfloat16),
            pltpu.VMEM((2, lines, width), jnp.bfloat16),
        ],
        compiler_params=params(32),
    )(x, *tables(lines, width))


def body(query, key_branch, value_branch, long_filter, skip_gain):
    channels, width = query.shape
    lines = lax.axis_size("grp") * lax.axis_size("pos")
    blocks = width // LANES
    sources = [
        pltpu.with_memory_space_constraint(x, pltpu.HBM)
        for x in (key_branch, value_branch, long_filter, skip_gain.reshape(1, channels))
    ]
    both = pl.pallas_call(
        gate_kernel,
        out_shape=pltpu.VMEM((channels, 2 * blocks, LANES), jnp.float32),
        in_specs=[pl.BlockSpec(memory_space=pltpu.HBM)] * 4,
        scratch_shapes=[
            pltpu.VMEM((channels, width), jnp.float32),
            pltpu.VMEM((channels, width), jnp.float32),
            pltpu.VMEM((1, channels), jnp.float32),
            pltpu.SemaphoreType.DMA((2, CHUNKS)),
            pltpu.SemaphoreType.DMA((blocks,)),
            pltpu.SemaphoreType.DMA,
        ],
        compiler_params=params(16),
    )(*sources)
    both = lax.all_to_all(both, AXES, split_axis=0, concat_axis=0, tiled=True)
    y = convolve(both.reshape(lines * 2 * blocks, LANES), lines, width)
    y = lax.all_to_all(y.reshape(lines, blocks, LANES), AXES, split_axis=0, concat_axis=0, tiled=True)
    return pl.pallas_call(
        mix_kernel,
        out_shape=jax.ShapeDtypeStruct((channels, width), jnp.float32),
        out_specs=pl.BlockSpec(memory_space=pltpu.HBM),
        scratch_shapes=[pltpu.VMEM((channels, width), jnp.float32), pltpu.SemaphoreType.DMA((CHUNKS,))],
        compiler_params=params(16),
    )(query, y.reshape(channels * blocks, LANES))


def solution(mesh):
    return jax.shard_map(
        body,
        mesh=mesh,
        in_specs=(P(None, AXES), P(None, AXES), P(None, AXES), P(None, AXES), P()),
        out_specs=P(None, AXES),
        check_vma=False,
    )
```

```python
import functools

import ml_dtypes
import numpy as np

import jax
import jax.numpy as jnp
from jax import lax
from jax.experimental import pallas as pl
from jax.experimental.pallas import tpu as pltpu
from jax.sharding import PartitionSpec as P

AXES = ("grp", "pos")
LANES = 128
RADIX = 4
CHUNKS = 2
STEP = 32


def params(mib):
    return pltpu.CompilerParams(vmem_limit_bytes=mib * 2**20)


def turns(numerator, denominator):
    angle = 2.0 * np.pi * (numerator % denominator) / denominator
    return np.cos(angle), np.sin(angle)


def high_low(table):
    high = table.astype(ml_dtypes.bfloat16)
    low = (table - high.astype(np.float64)).astype(ml_dtypes.bfloat16)
    return high, low


def table_pair(table, axis):
    return np.concatenate(high_low(table), axis)


@functools.lru_cache
def tables(lines, width):
    length = lines * width
    line = np.arange(lines)
    offset = np.arange(width)
    half = line[: lines // 2]
    first, last = [], []
    for j in range(2):
        ch, sh = turns(np.outer(4 * half + 1, 2 * half + j), 4 * lines)
        first.append(table_pair(np.concatenate([ch, -sh], 0), -1))
        ch, sh = turns(np.outer(2 * half + j, 4 * half + 1), 4 * lines)
        last.append(table_pair(np.concatenate([ch, -sh], 1), -1))
    ct, st = turns(np.outer(4 * line + 1, offset), 4 * length)
    small = np.arange(width // RADIX)
    forth, back = [], []
    for r in range(RADIX):
        c2, s2 = turns(np.outer(small, RADIX * small + r), width)
        block = np.block([[c2, -s2], [s2, c2]])
        forth.append(block)
        back.append(block.T / length)
    return (
        np.stack(first),
        np.concatenate([ct, st], 0).astype(np.float32),
        table_pair(np.stack(forth), -2),
        table_pair(np.stack(back), -2),
        np.stack(last),
    )


def split(x):
    high = x.astype(jnp.bfloat16)
    return high, (x - high.astype(jnp.float32)).astype(jnp.bfloat16)


def dot(a, b):
    return jnp.dot(a, b, preferred_element_type=jnp.float32)


def dot_left(table, high, low):
    depth = high.shape[0]
    table = jnp.concatenate([table, table[:, :depth]], 1)
    return dot(table, jnp.concatenate([high, high, low], 0))


def dot_right(high, low, table):
    depth = high.shape[1]
    table = jnp.concatenate([table, table[:depth]], 0)
    return dot(jnp.concatenate([high, high, low], 1), table)


def gate_kernel(key_hbm, value_hbm, filter_hbm, skip_hbm, out_ref, key_ref, value_ref, skip_ref, sems, filter_sems, skip_sem):
    channels, width = key_ref.shape
    blocks = width // LANES
    part = channels // CHUNKS
    flat = out_ref.reshape(channels * 2 * blocks, LANES)

    def copies(i):
        rows = pl.ds(i * part, part)
        pairs = ((key_hbm, key_ref), (value_hbm, value_ref))
        return [
            pltpu.make_async_copy(there.at[rows], here.at[rows], sems.at[n, i]) for n, (there, here) in enumerate(pairs)
        ]

    for i in range(CHUNKS):
        for copy in copies(i):
            copy.start()
    filter_copies = [
        pltpu.make_async_copy(
            filter_hbm.at[:, pl.ds(q * LANES, LANES)], out_ref.at[:, blocks + q, :], filter_sems.at[q]
        )
        for q in range(blocks)
    ]
    for copy in filter_copies:
        copy.start()
    skip_copy = pltpu.make_async_copy(skip_hbm, skip_ref, skip_sem)
    skip_copy.start()
    for i in range(CHUNKS):
        for copy in copies(i):
            copy.wait()
        rows = pl.ds(i * part, part)
        for q in range(blocks):
            at = pl.ds(q * LANES, LANES)
            flat[pl.ds(i * part * 2 * blocks + q, part, stride=2 * blocks), :] = key_ref[rows, at] * value_ref[rows, at]
    skip_copy.wait()
    for copy in filter_copies:
        copy.wait()

    @pl.when((lax.axis_index(AXES[0]) == 0) & (lax.axis_index(AXES[1]) == 0))
    def _():
        lane = lax.broadcasted_iota(jnp.int32, (channels, LANES), 1)
        skip = jnp.broadcast_to(skip_ref[...], (LANES, channels)).T
        at = pl.ds(blocks, channels, stride=2 * blocks)
        flat[at, :] = flat[at, :] + jnp.where(lane == 0, skip, 0.0)


def four(pairs, sign):
    (ar, ai), (br, bi), (cr, ci), (dr, di) = pairs
    e0r, e0i, e1r, e1i = ar + cr, ai + ci, ar - cr, ai - ci
    o0r, o0i, o1r, o1i = br + dr, bi + di, br - dr, bi - di
    turned, other = (e1r - o1i, e1i + o1r), (e1r + o1i, e1i - o1r)
    if sign < 0:
        turned, other = other, turned
    return (e0r + o0r, e0i + o0i), turned, (e0r - o0r, e0i - o0i), other


def convolve_kernel(x_ref, first_ref, twist_ref, forth_ref, back_ref, last_ref, y_ref, xh, xl, zh, zl, dh, dl):
    lines = y_ref.shape[0] // RADIX
    width = RADIX * LANES
    half = lines // 2

    def lanes(q):
        return slice(q * LANES, (q + 1) * LANES)

    def take(signal):
        for q in range(RADIX):
            n = signal * RADIX + q
            for j in range(2):
                at = slice(j * half, (j + 1) * half)
                xh[at, lanes(n)], xl[at, lanes(n)] = split(
                    x_ref[pl.ds(2 * RADIX * j + n, half, stride=4 * RADIX), :]
                )

    def over_lines(signal):
        at = slice(signal * width, (signal + 1) * width)
        spread = []
        for j in range(2):
            rows = slice(j * half, (j + 1) * half)
            spread.append(dot_left(first_ref[j], xh[rows, at], xl[rows, at]))
        return spread

    def turn(signal, spread, start=0, stop=lines):
        even, odd = spread
        for row in range(start, stop, STEP):
            here = slice(signal * lines + row, signal * lines + row + STEP)
            k = row % half
            pairs = []
            for q in range(RADIX):
                er, ei = even[k : k + STEP, lanes(q)], even[half + k : half + k + STEP, lanes(q)]
                fr, fi = odd[k : k + STEP, lanes(q)], odd[half + k : half + k + STEP, lanes(q)]
                re, im = (er + fr, ei + fi) if row < half else (er - fr, ei - fi)
                ct, st = twist_ref[row : row + STEP, lanes(q)], twist_ref[lines + row : lines + row + STEP, lanes(q)]
                pairs.append((re * ct + im * st, im * ct - re * st))
            for r, pair in enumerate(four(pairs, -1)):
                for part, value in enumerate(pair):
                    zh[r, here, lanes(part)], zl[r, here, lanes(part)] = split(value)

    def over_offsets(signal, r):
        at = slice(signal * lines, (signal + 1) * lines)
        return dot_right(zh[r, at], zl[r, at], forth_ref[r])

    def product(g, f):
        gr, gi, fr, fi = g[:, :LANES], g[:, LANES:], f[:, :LANES], f[:, LANES:]
        return split(jnp.concatenate([gr * fr - gi * fi, gr * fi + gi * fr], 1))

    def turned_back(backs, row):
        pairs = [(back[row : row + STEP, :LANES], back[row : row + STEP, LANES:]) for back in backs]
        turned = []
        for q, (re, im) in enumerate(four(pairs, 1)):
            ct = twist_ref[row : row + STEP, lanes(q)]
            st = twist_ref[lines + row : lines + row + STEP, lanes(q)]
            turned.append((re * ct - im * st, im * ct + re * st))
        return turned

    def turn_back(backs):
        later = []
        for row in range(0, half, STEP):
            both = zip(turned_back(backs, row), turned_back(backs, half + row))
            for q, (near, far) in enumerate(both):
                for part in range(2):
                    at = slice(part * half + row, part * half + row + STEP)
                    dh[0, at, lanes(q)], dl[0, at, lanes(q)] = split(near[part] + far[part])
                    later.append((at, lanes(q), near[part] - far[part]))
        return later

    take(0)
    spread_g = over_lines(0)
    take(1)
    spread_f = over_lines(1)
    turn(0, spread_g)
    gs = []
    for r in range(RADIX):
        turn(1, spread_f, r * lines // RADIX, (r + 1) * lines // RADIX)
        gs.append(over_offsets(0, r))
    fs = [over_offsets(1, r) for r in range(RADIX)]
    backs = []
    for r in range(RADIX):
        parts = []
        for k in range(0, lines, half):
            rows = slice(k, k + half)
            high, low = product(gs[r][rows], fs[r][rows])
            parts.append(dot_right(high, low, back_ref[r]))
        backs.append(jnp.concatenate(parts, 0))
    later = turn_back(backs)
    for j in range(2):
        y = dot_left(last_ref[j], dh[j], dl[j])
        if j == 0:
            for rows, at, value in later:
                dh[1, rows, at], dl[1, rows, at] = split(value)
        for q in range(RADIX):
            y_ref[pl.ds(j * RADIX + q, half, stride=2 * RADIX), :] = y[:, lanes(q)]


def mix_kernel(query_ref, y_ref, out_hbm, out_ref, sems):
    channels, width = query_ref.shape
    blocks = width // LANES
    part = channels // CHUNKS
    copies = []
    for i in range(CHUNKS):
        rows = pl.ds(i * part, part)
        for q in range(blocks):
            at = pl.ds(q * LANES, LANES)
            out_ref[rows, at] = query_ref[rows, at] * y_ref[pl.ds(i * part * blocks + q, part, stride=blocks), :]
        copies.append(pltpu.make_async_copy(out_ref.at[rows], out_hbm.at[rows], sems.at[i]))
        copies[-1].start()
    for copy in copies:
        copy.wait()


def convolve(x, lines, width):
    return pl.pallas_call(
        convolve_kernel,
        out_shape=jax.ShapeDtypeStruct((lines * RADIX, LANES), jnp.float32),
        scratch_shapes=[
            pltpu.VMEM((lines, 2 * width), jnp.bfloat16),
            pltpu.VMEM((lines, 2 * width), jnp.bfloat16),
            pltpu.VMEM((RADIX, 2 * lines, 2 * LANES), jnp.bfloat16),
            pltpu.VMEM((RADIX, 2 * lines, 2 * LANES), jnp.bfloat16),
            pltpu.VMEM((2, lines, width), jnp.bfloat16),
            pltpu.VMEM((2, lines, width), jnp.bfloat16),
        ],
        compiler_params=params(32),
    )(x, *tables(lines, width))


def body(query, key_branch, value_branch, long_filter, skip_gain):
    channels, width = query.shape
    lines = lax.axis_size("grp") * lax.axis_size("pos")
    blocks = width // LANES
    sources = [
        pltpu.with_memory_space_constraint(x, pltpu.HBM)
        for x in (key_branch, value_branch, long_filter, skip_gain.reshape(1, channels))
    ]
    both = pl.pallas_call(
        gate_kernel,
        out_shape=pltpu.VMEM((channels, 2 * blocks, LANES), jnp.float32),
        in_specs=[pl.BlockSpec(memory_space=pltpu.HBM)] * 4,
        scratch_shapes=[
            pltpu.VMEM((channels, width), jnp.float32),
            pltpu.VMEM((channels, width), jnp.float32),
            pltpu.VMEM((1, channels), jnp.float32),
            pltpu.SemaphoreType.DMA((2, CHUNKS)),
            pltpu.SemaphoreType.DMA((blocks,)),
            pltpu.SemaphoreType.DMA,
        ],
        compiler_params=params(16),
    )(*sources)
    both = lax.all_to_all(both, AXES, split_axis=0, concat_axis=0, tiled=True)
    y = convolve(both.reshape(lines * 2 * blocks, LANES), lines, width)
    y = lax.all_to_all(y.reshape(lines, blocks, LANES), AXES, split_axis=0, concat_axis=0, tiled=True)
    return pl.pallas_call(
        mix_kernel,
        out_shape=jax.ShapeDtypeStruct((channels, width), jnp.float32),
        out_specs=pl.BlockSpec(memory_space=pltpu.HBM),
        scratch_shapes=[pltpu.VMEM((channels, width), jnp.float32), pltpu.SemaphoreType.DMA((CHUNKS,))],
        compiler_params=params(16),
    )(query, y.reshape(channels * blocks, LANES))


def solution(mesh):
    return jax.shard_map(
        body,
        mesh=mesh,
        in_specs=(P(None, AXES), P(None, AXES), P(None, AXES), P(None, AXES), P()),
        out_specs=P(None, AXES),
        check_vma=False,
    )
```
